32 devices in a mesh: gx: 8 (over z, y), gy: 4 (over x, core).
Axes of the slice: x: 2, y: 2, z: 4, core: 2. Of those that a mesh axis runs over, the one named last changes fastest.
Arguments:
- flux_perturbation: float32 [2, 4096, 4096], P(None, 'gx', 'gy'), may hold values from -6 to 6
- archived_nominal_heat_levels: float32 [2, 2, 4096, 4096], P(None, None, 'gx', 'gy'), may hold values from -4 to 4
- archived_solidity_labels: int32 [2, 2, 4096, 4096], P(None, None, 'gx', 'gy'), may hold values from 0 to 2
Outputs:
- hess_vec: float32 [2, 4096, 4096], P(None, 'gx', 'gy')
The draws below stay inside these ranges and needn't reach their ends.
Inputs may be any that keep to these rules, and one draw needn't show every extreme that they name: `archived_solidity_labels`: 0 is solid, 1 mushy, 2 liquid.
All inputs are finite; a program needn't handle non-finite values.
Results may differ from the reference program's by a relative error of at most 0.000061.
Values sent between devices are 32-bit elements; how exact they have to be, the bound alone decides.
A program may use at most 192 MiB of HBM per device.

```python
import math
import jax
import jax.numpy as jnp
from jax import lax

NVEC = 2
MESH_LENGTHWISE = 4096
MESH_TRANSVERSE = 4096
SUBSURFACE_TIERS = 2
ARCHIVED_MOMENTS = 2


def draw_flux_perturbation(key, part):
    keys = jax.random.split(key, 4)
    modes = 4
    low_x = MESH_LENGTHWISE // 384 + 1
    high_x = MESH_LENGTHWISE // 64 + 1
    low_y = MESH_TRANSVERSE // 384 + 1
    high_y = MESH_TRANSVERSE // 64 + 1
    freq_x = jax.random.randint(keys[0], (NVEC, 3, modes), low_x, high_x)
    freq_y = jax.random.randint(keys[1], (NVEC, 3, modes), low_y, high_y)
    phase = jax.random.uniform(keys[2], (NVEC, 3, modes), jnp.float32, 0.0, 2.0 * math.pi)
    pos_x = jnp.arange(MESH_LENGTHWISE, dtype=jnp.int32)
    pos_y = jnp.arange(MESH_TRANSVERSE, dtype=jnp.int32)
    angle_x = (freq_x[..., None] * pos_x % MESH_LENGTHWISE).astype(jnp.float32) * (2.0 * math.pi / MESH_LENGTHWISE) + phase[..., None]
    angle_y = (freq_y[..., None] * pos_y % MESH_TRANSVERSE).astype(jnp.float32) * (2.0 * math.pi / MESH_TRANSVERSE)
    cos_x = jnp.cos(angle_x)
    sin_x = jnp.sin(angle_x)
    cos_y = jnp.cos(angle_y)
    sin_y = jnp.sin(angle_y)
    sign_x = (1 - 2 * (pos_x % 2)).astype(jnp.float32)
    sign_y = (1 - 2 * (pos_y % 2)).astype(jnp.float32)
    unit_x = jnp.ones((MESH_LENGTHWISE,), jnp.float32)
    unit_y = jnp.ones((MESH_TRANSVERSE,), jnp.float32)
    base = jax.random.normal(keys[3], (NVEC, MESH_LENGTHWISE, MESH_TRANSVERSE), jnp.float32)
    amplitude = 1.5
    weight = amplitude * math.sqrt(2.0 / modes)
    pattern_x = (sign_x, unit_x, sign_x)
    pattern_y = (unit_y, sign_y, sign_y)
    total = base
    for pattern in range(3):
        envelope = jnp.zeros((NVEC, MESH_LENGTHWISE, MESH_TRANSVERSE), jnp.float32)
        for mode in range(modes):
            envelope = envelope + cos_x[:, pattern, mode][:, :, None] * cos_y[:, pattern, mode][:, None, :]
            envelope = envelope - sin_x[:, pattern, mode][:, :, None] * sin_y[:, pattern, mode][:, None, :]
        total = total + weight * envelope * pattern_x[pattern][None, :, None] * pattern_y[pattern][None, None, :]
    return jnp.clip(total, -6.0, 6.0).astype(jnp.float32)


def place_ends(drawn, stream_key, smallest, largest):
    longest = drawn.shape.index(max(drawn.shape))
    spots = []
    for shift in (0, 1):
        where = [jax.random.randint(jax.random.fold_in(stream_key, axis), (), 0, length) for axis, length in enumerate(drawn.shape)]
        where[longest] = (where[longest] + shift) % drawn.shape[longest]
        spots.append(tuple(where))
    return drawn.at[spots[0]].set(smallest).at[spots[1]].set(largest)


def levels(key, shape, cuts, low, high):
    loudness, own = 1.0, jax.random.fold_in(key, 6)
    for position, blocks in cuts:
        draws = jnp.exp(jax.random.uniform(jax.random.fold_in(own, position), (blocks,), jnp.float32, low / len(cuts), high / len(cuts)))
        loudness = loudness * jnp.repeat(draws, shape[position] // blocks).reshape([-1 if axis == position else 1 for axis in range(len(shape))])
    return loudness


def scatter_about(rng, dims, scale, most, cuts=(), kind=jnp.bfloat16):
    result = scale * jax.random.normal(rng, dims, jnp.float32)
    if cuts:
        result = result * levels(rng, dims, cuts, -0.22, 0.18)
    return jnp.clip(result, -most, most).astype(kind)


def setup_inputs(seed: int = 0) -> dict:
    key_list = jax.random.split(jax.random.key(seed), 4)
    return {
        "flux_perturbation": draw_flux_perturbation(jax.random.fold_in(key_list[3], 71), 0),
        "archived_nominal_heat_levels": scatter_about(key_list[1], (ARCHIVED_MOMENTS, SUBSURFACE_TIERS, MESH_LENGTHWISE, MESH_TRANSVERSE), 1.0, 4.0, ((2, 8), (3, 4)), jnp.float32),
        "archived_solidity_labels": place_ends(jax.random.randint(key_list[2], (ARCHIVED_MOMENTS, SUBSURFACE_TIERS, MESH_LENGTHWISE, MESH_TRANSVERSE), 0, 3), jax.random.fold_in(key_list[2], 1), 0, 2).astype(jnp.int32),
    }


TIME_STEP = 0.1
OBS_WEIGHT = 10.0
PRIOR_GAIN = 0.005


def laplace(field):
    padded = jnp.pad(field, 1)
    total = padded[2:, 1:-1, 1:-1] + padded[:-2, 1:-1, 1:-1]
    total = total + padded[1:-1, 2:, 1:-1] + padded[1:-1, :-2, 1:-1]
    total = total + padded[1:-1, 1:-1, 2:] + padded[1:-1, 1:-1, :-2]
    return total - 6.0 * field


def reference(flux_perturbation, archived_nominal_heat_levels, archived_solidity_labels):
    capacity = jnp.where(archived_solidity_labels == 0, 1.0, jnp.where(archived_solidity_labels == 1, 4.0, 1.25)).astype(jnp.float32)
    diffusion_advance = jnp.where(archived_solidity_labels == 0, 1.0, jnp.where(archived_solidity_labels == 1, 0.6, 0.35)).astype(jnp.float32)
    diffusion_advance = diffusion_advance * (1.0 + 0.5 * jnp.tanh(archived_nominal_heat_levels))
    wave_x = (2.0 * math.pi * jnp.fft.fftfreq(MESH_LENGTHWISE)) ** 2
    wave_y = (2.0 * math.pi * jnp.fft.fftfreq(MESH_TRANSVERSE)) ** 2
    symbol = PRIOR_GAIN * (wave_x[:, None] + wave_y[None, :]) ** 2

    def single(vector):
        zero_layer = jnp.zeros_like(vector)
        source = jnp.stack([vector, zero_layer])
        first_h = TIME_STEP * source
        second_h = first_h + TIME_STEP * (diffusion_advance[0] * laplace(first_h / capacity[0]) + source)
        third_h = second_h + TIME_STEP * (diffusion_advance[1] * laplace(second_h / capacity[1]) + source)
        misfit = OBS_WEIGHT * third_h[0] / capacity[1, 0]
        adj_three = jnp.stack([misfit / capacity[1, 0], zero_layer])
        adj_two = adj_three + laplace(TIME_STEP * diffusion_advance[1] * adj_three) / capacity[1]
        adj_one = adj_two + laplace(TIME_STEP * diffusion_advance[0] * adj_two) / capacity[0]
        data_term = TIME_STEP * (adj_three[0] + adj_two[0] + adj_one[0])
        prior_term = jnp.real(jnp.fft.ifft2(jnp.fft.fft2(vector) * symbol))
        return (data_term + prior_term).astype(jnp.float32)

    return lax.map(single, flux_perturbation)
```

```python
import math

import jax
import jax.numpy as jnp
import numpy as np
from jax import lax
from jax.experimental import pallas as pl
from jax.experimental.pallas import tpu as pltpu
from jax.sharding import PartitionSpec as P

TIME_STEP = 0.1
OBS_WEIGHT = 10.0
PRIOR_GAIN = 0.005
HIGHEST = lax.Precision.HIGHEST


def with_halo(cells, sides, width):
    for axis, dim in sides:
        count = lax.axis_size(axis)
        ends = count - 1
        head = lax.slice_in_dim(cells, 0, width, axis=dim)
        tail = lax.slice_in_dim(cells, cells.shape[dim] - width, cells.shape[dim], axis=dim)
        cells = jnp.concatenate(
            [
                lax.ppermute(tail, axis, [(i, (i + 1) % count) for i in range(ends)]),
                cells,
                lax.ppermute(head, axis, [((i + 1) % count, i) for i in range(ends)]),
            ],
            axis=dim,
        )
    return cells


def surface_rim(field):
    padded = with_halo(field, (("gx", 1), ("gy", 2)), 1)
    return padded[:, 2:, 1:-1] + padded[:, :-2, 1:-1] + padded[:, 1:-1, 2:] + padded[:, 1:-1, :-2]


def cos_sin(horizontal_line_total, col_count, modulus):
    row_ids = jnp.arange(horizontal_line_total, dtype=jnp.int32)[:, None]
    col_ids = jnp.arange(col_count, dtype=jnp.int32)[None, :]
    angles = (row_ids * col_ids % modulus).astype(jnp.float32) * (2.0 * math.pi / modulus)
    return (jnp.cos(angles), jnp.sin(angles))


def tables(length):
    bit_count = length.bit_length() - 1
    outer_len = 2 ** (bit_count // 2)
    inner_len = length // outer_len
    cos_outer, sin_outer = cos_sin(outer_len, outer_len, outer_len)
    cos_inner, sin_inner = cos_sin(inner_len, inner_len, inner_len)
    twist_cos, twist_sin = cos_sin(outer_len, inner_len, length)
    outer_fwd = jnp.stack([cos_outer, -sin_outer])
    inner_fwd = jnp.stack([jnp.stack([cos_inner, -sin_inner]), jnp.stack([sin_inner, cos_inner])])
    inner_inv = jnp.stack([jnp.stack([cos_inner, sin_inner]), jnp.stack([-sin_inner, cos_inner])])
    outer_inv = jnp.stack([cos_outer, -sin_outer])
    freq_index = (
        jnp.arange(outer_len, dtype=jnp.int32)[:, None]
        + outer_len * jnp.arange(inner_len, dtype=jnp.int32)[None, :]
    )
    signed = jnp.where(freq_index < length // 2, freq_index, freq_index - length).astype(
        jnp.float32
    )
    wave_sq = (signed * (2.0 * math.pi / length)) ** 2
    return (
        length,
        outer_len,
        inner_len,
        outer_fwd,
        inner_fwd,
        inner_inv,
        outer_inv,
        twist_cos,
        twist_sin,
        wave_sq,
    )


def forward(field, table):
    (
        length,
        outer_len,
        inner_len,
        outer_fwd,
        inner_fwd,
        inner_inv,
        outer_inv,
        twist_cos,
        twist_sin,
        wave_sq,
    ) = table
    grid = field.reshape(field.shape[:-1] + (outer_len, inner_len))
    stepped = jnp.einsum("...ab,rak->...rkb", grid, outer_fwd, precision=HIGHEST)
    step_re = stepped[..., 0, :, :]
    step_im = stepped[..., 1, :, :]
    twisted = jnp.stack(
        [step_re * twist_cos + step_im * twist_sin, step_im * twist_cos - step_re * twist_sin],
        axis=-3,
    )
    spec = jnp.einsum("...rkb,rsbm->...skm", twisted, inner_fwd, precision=HIGHEST)
    return (spec[..., 0, :, :], spec[..., 1, :, :])


def inverse(spec_re, spec_im, table):
    (
        length,
        outer_len,
        inner_len,
        outer_fwd,
        inner_fwd,
        inner_inv,
        outer_inv,
        twist_cos,
        twist_sin,
        wave_sq,
    ) = table
    stacked = jnp.stack([spec_re, spec_im], axis=-3)
    halved = jnp.einsum("...skm,srbm->...rkb", stacked, inner_inv, precision=HIGHEST)
    half_re = halved[..., 0, :, :]
    half_im = halved[..., 1, :, :]
    turned = jnp.stack(
        [half_re * twist_cos - half_im * twist_sin, half_im * twist_cos + half_re * twist_sin],
        axis=-3,
    )
    grid = jnp.einsum("...rkb,rka->...ab", turned, outer_inv, precision=HIGHEST)
    return grid.reshape(grid.shape[:-2] + (length,)) / length


def shards_general(flux_perturbation, archived_nominal_heat_levels, archived_solidity_labels):
    capacity = jnp.where(
        archived_solidity_labels == 0, 1.0, jnp.where(archived_solidity_labels == 1, 4.0, 1.25)
    ).astype(jnp.float32)
    diffusion_advance = jnp.where(
        archived_solidity_labels == 0, 1.0, jnp.where(archived_solidity_labels == 1, 0.6, 0.35)
    ).astype(jnp.float32)
    diffusion_advance = diffusion_advance * (1.0 + 0.5 * jnp.tanh(archived_nominal_heat_levels))
    rows = lax.all_to_all(flux_perturbation, "gx", split_axis=2, concat_axis=1, tiled=True)
    row_table = tables(rows.shape[1])
    first_u = TIME_STEP * flux_perturbation / capacity[0, 0]
    second_top = TIME_STEP * flux_perturbation + TIME_STEP * (
        diffusion_advance[0, 0] * (surface_rim(first_u) - 6.0 * first_u) + flux_perturbation
    )
    second_low = TIME_STEP * diffusion_advance[0, 1] * first_u
    top_u = second_top / capacity[1, 0]
    low_u = second_low / capacity[1, 1]
    third_top = second_top + TIME_STEP * (
        diffusion_advance[1, 0] * (surface_rim(top_u) - 6.0 * top_u + low_u) + flux_perturbation
    )
    misfit = OBS_WEIGHT * third_top / capacity[1, 0]
    adj_three = misfit / capacity[1, 0]
    push_top = TIME_STEP * diffusion_advance[1, 0] * adj_three
    adj_two_top = adj_three + (surface_rim(push_top) - 6.0 * push_top) / capacity[1, 0]
    adj_two_low = push_top / capacity[1, 1]
    pull_top = TIME_STEP * diffusion_advance[0, 0] * adj_two_top
    pull_low = TIME_STEP * diffusion_advance[0, 1] * adj_two_low
    adj_one_top = adj_two_top + (surface_rim(pull_top) - 6.0 * pull_top + pull_low) / capacity[0, 0]
    data_term = TIME_STEP * (adj_three + adj_two_top + adj_one_top)
    row_re, row_im = forward(jnp.swapaxes(rows, 1, 2), row_table)
    wave_x = row_table[-1]
    second_x = jnp.swapaxes(
        inverse(2.0 * PRIOR_GAIN * wave_x * row_re, 2.0 * PRIOR_GAIN * wave_x * row_im, row_table),
        1,
        2,
    )
    fourth_x = jnp.swapaxes(
        inverse(
            PRIOR_GAIN * wave_x * wave_x * row_re, PRIOR_GAIN * wave_x * wave_x * row_im, row_table
        ),
        1,
        2,
    )
    second_back, fourth_part = (
        lax.all_to_all(second_x, "gx", split_axis=1, concat_axis=2, tiled=True),
        lax.all_to_all(fourth_x, "gx", split_axis=1, concat_axis=2, tiled=True),
    )
    cols_dir, cols_second = (
        lax.all_to_all(flux_perturbation, "gy", split_axis=1, concat_axis=2, tiled=True),
        lax.all_to_all(second_back, "gy", split_axis=1, concat_axis=2, tiled=True),
    )
    col_table = tables(cols_dir.shape[2])
    dir_re, dir_im = forward(cols_dir, col_table)
    sec_re, sec_im = forward(cols_second, col_table)
    wave_y = col_table[-1]
    mixed = inverse(
        PRIOR_GAIN * wave_y * wave_y * dir_re + wave_y * sec_re,
        PRIOR_GAIN * wave_y * wave_y * dir_im + wave_y * sec_im,
        col_table,
    )
    mixed_back = lax.all_to_all(mixed, "gy", split_axis=2, concat_axis=1, tiled=True)
    return data_term + fourth_part + mixed_back


OUTER = 16


def half_spectrum(xs):
    n = len(xs)
    if n == 2:
        return [(xs[0] + xs[1], None), (xs[0] - xs[1], None)]
    even, odd = half_spectrum(xs[0::2]), half_spectrum(xs[1::2])
    out = [None] * (n // 2 + 1)
    for k in range(n // 4 + 1):
        er, ei = even[k]
        orr, oi = odd[k]
        if k == 0:
            out[0] = (er + orr, None)
            out[n // 2] = (er - orr, None)
        elif k == n // 4:
            out[k] = (er, -orr)
        else:
            c, s = math.cos(2 * math.pi * k / n), math.sin(2 * math.pi * k / n)
            if 8 * k == n:
                tr, ti = c * (orr + oi), c * (oi - orr)
            else:
                tr, ti = c * orr + s * oi, c * oi - s * orr
            out[k] = (er + tr, ei + ti)
            out[n // 2 - k] = (er - tr, ti - ei)
    return out


def half_spectrum_t(gs):
    half = len(gs) - 1
    n = 2 * half
    if n == 2:
        return [gs[0][0] + gs[1][0], gs[0][0] - gs[1][0]]
    even, odd = [], []
    for m in range(n // 4 + 1):
        gr, gi = gs[m]
        if m == 0:
            hr = gs[half][0]
            even.append((gr + hr, None))
            odd.append((gr - hr, None))
        elif m == n // 4:
            even.append((gr, None))
            odd.append((-gi, None))
        else:
            hr, hi = gs[half - m]
            even.append((gr + hr, gi - hi))
            dr, di = gr - hr, gi + hi
            c, s = math.cos(2 * math.pi * m / n), math.sin(2 * math.pi * m / n)
            if 8 * m == n:
                odd.append((c * (dr - di), c * (dr + di)))
            else:
                odd.append((c * dr - s * di, c * di + s * dr))
    out = [None] * n
    out[0::2] = half_spectrum_t(even)
    out[1::2] = half_spectrum_t(odd)
    return out


def line_tables(length):
    inner = length // OUTER
    groups = OUTER // 2
    b = np.arange(inner)[:, None]
    mats = np.zeros((groups, 2 * inner, 2 * inner))
    freq = np.zeros((groups, 2 * inner), np.int64)
    scale = math.sqrt(2.0 / length)
    for k1 in range(1, groups):
        k = k1 + OUTER * np.arange(inner)
        angle = 2.0 * math.pi * ((b * k[None, :]) % length) / length
        c, s = np.cos(angle) * scale, np.sin(angle) * scale
        mats[k1 - 1] = np.block([[c, -s], [s, c]])
        freq[k1 - 1] = np.concatenate([k, k])
    last = groups - 1
    for part, first in ((0, 0), (1, groups)):
        k = first + OUTER * np.arange(inner // 2)
        angle = 2.0 * math.pi * ((b * k[None, :]) % length) / length
        c, s = np.cos(angle) * scale, np.sin(angle) * scale
        k_sin = k.copy()
        if first == 0:
            c[:, 0] = math.sqrt(1.0 / length)
            k_sin[0] = length // 2
            s[:, 0] = -math.sqrt(1.0 / length) * (1 - 2 * (np.arange(inner) % 2))
        span = slice(part * inner, (part + 1) * inner)
        mats[last][span, span] = np.concatenate([c, -s], axis=1)
        freq[last][span] = np.concatenate([k, k_sin])
    signed = np.where(freq < length // 2, freq, freq - length)
    wave = (signed * (2.0 * math.pi / length)) ** 2
    return mats, wave


def two_parts(mats):
    top = np.asarray(mats, np.float32).astype(jnp.bfloat16)
    rest = (np.asarray(mats, np.float64) - top.astype(np.float64)).astype(jnp.bfloat16)
    return top, rest


def split(x):
    top = x.astype(jnp.bfloat16)
    return top, (x - top.astype(jnp.float32)).astype(jnp.bfloat16)


def dot32(a, b):
    return jnp.dot(a, b, preferred_element_type=jnp.float32)


def right(x, hi, lo):
    top, rest = split(x)
    return dot32(top, hi) + (dot32(rest, hi) + dot32(top, lo))


def left(hi, lo, x):
    top, rest = split(x)
    return dot32(hi, top) + (dot32(lo, top) + dot32(hi, rest))


def pairs(spec):
    ends = len(spec) - 1
    return [spec[k] for k in range(1, ends)] + [(spec[0][0], spec[ends][0])]


def unpairs(groups):
    return [(groups[-1][0], None)] + groups[:-1] + [(groups[-1][1], None)]


def y_forward(x_ref, hi_ref, lo_ref, out_ref):
    parts, wide = x_ref.shape[0], x_ref.shape[-1]
    inner = parts * wide // OUTER
    per = wide // inner
    xs = [x_ref[a // per, 0, :, (a % per) * inner : (a % per + 1) * inner] for a in range(OUTER)]
    width = out_ref.shape[-1]
    each = 2 * inner // width
    for g, (re, im) in enumerate(pairs(half_spectrum(xs))):
        res = right(jnp.concatenate([re, im], axis=1), hi_ref[g], lo_ref[g])
        for c in range(each):
            out_ref[g * each + c, 0] = res[:, c * width : (c + 1) * width]


def y_inverse(x_ref, hi_ref, lo_ref, out_ref):
    parts, wide = out_ref.shape[0], out_ref.shape[-1]
    inner = parts * wide // OUTER
    per = wide // inner
    width = x_ref.shape[-1]
    each = 2 * inner // width
    groups = []
    for g in range(OUTER // 2):
        spec = jnp.concatenate([x_ref[g * each + c, 0] for c in range(each)], axis=1)
        res = right(spec, hi_ref[g], lo_ref[g])
        groups.append((res[:, :inner], res[:, inner:]))
    for a, slab in enumerate(half_spectrum_t(unpairs(groups))):
        out_ref[a // per, 0, :, (a % per) * inner : (a % per + 1) * inner] = slab


def x_apply(x_ref, ky_ref, kx_ref, fhi_ref, flo_ref, ihi_ref, ilo_ref, out_ref):
    count, nvec, rows, width = x_ref.shape
    inner = count * rows // OUTER
    per = inner // rows

    def slab(a):
        return jnp.concatenate(
            [x_ref[a * per : (a + 1) * per, v].reshape(inner, width) for v in range(nvec)], axis=1
        )

    ky = jnp.concatenate([ky_ref[...]] * nvec, axis=1)
    groups = []
    for g, (re, im) in enumerate(pairs(half_spectrum([slab(a) for a in range(OUTER)]))):
        spec = left(fhi_ref[g], flo_ref[g], jnp.concatenate([re, im], axis=0))
        wave = kx_ref[g] + ky
        res = left(ihi_ref[g], ilo_ref[g], PRIOR_GAIN * wave * wave * spec)
        groups.append((res[:inner], res[inner:]))
    for a, res in enumerate(half_spectrum_t(unpairs(groups))):
        for v in range(nvec):
            out_ref[a * per : (a + 1) * per, v] = res[:, v * width : (v + 1) * width].reshape(
                per, rows, width
            )


def prior(q):
    across, along = lax.axis_size("gx"), lax.axis_size("gy")
    nvec, bx, by = q.shape
    length = by * along
    count = across * along
    rows = bx // along
    width = length // count
    mats, wave = line_tables(length)
    fhi, flo = two_parts(mats)
    thi, tlo = two_parts(np.swapaxes(mats, 1, 2))
    params = pltpu.CompilerParams(vmem_limit_bytes=58 * 2**20)
    table = pl.BlockSpec(fhi.shape, lambda v: (0, 0, 0))
    lines = pl.BlockSpec((along, 1, rows, by), lambda v: (0, v, 0, 0))
    packed = pl.BlockSpec((count, 1, rows, width), lambda v: (0, v, 0, 0))
    lines_shape = jax.ShapeDtypeStruct((along, nvec, rows, by), jnp.float32)
    packed_shape = jax.ShapeDtypeStruct((count, nvec, rows, width), jnp.float32)

    send = jnp.swapaxes(q.reshape(nvec, along, rows, by), 0, 1)
    whole_y = lax.all_to_all(send, "gy", 0, 0, tiled=True)
    spec_y = pl.pallas_call(
        y_forward, grid=(nvec,), in_specs=[lines, table, table], out_specs=packed,
        out_shape=packed_shape, compiler_params=params, name="y_forward",
    )(whole_y, fhi, flo)
    whole_x = lax.all_to_all(spec_y, ("gx", "gy"), 0, 0, tiled=True)
    me = lax.axis_index("gx") * along + lax.axis_index("gy")
    ky = lax.dynamic_slice_in_dim(
        jnp.asarray(wave.reshape(1, length), jnp.float32), me * width, width, axis=1
    )
    kx = jnp.asarray(wave[:, :, None], jnp.float32)
    done_x = pl.pallas_call(
        x_apply, out_shape=packed_shape, compiler_params=params, name="x_apply",
    )(whole_x, ky, kx, thi, tlo, fhi, flo)
    back_y = lax.all_to_all(done_x, ("gx", "gy"), 0, 0, tiled=True)
    done_y = pl.pallas_call(
        y_inverse, grid=(nvec,), in_specs=[packed, table, table], out_specs=lines,
        out_shape=lines_shape, compiler_params=params, name="y_inverse",
    )(back_y, thi, tlo)
    back = lax.all_to_all(done_y, "gy", 0, 0, tiled=True)
    return jnp.swapaxes(back, 0, 1).reshape(nvec, bx, by)


def data_term(flux_perturbation, archived_nominal_heat_levels, archived_solidity_labels):
    capacity = jnp.where(
        archived_solidity_labels == 0, 1.0, jnp.where(archived_solidity_labels == 1, 4.0, 1.25)
    ).astype(jnp.float32)
    diffusion_advance = jnp.where(
        archived_solidity_labels == 0, 1.0, jnp.where(archived_solidity_labels == 1, 0.6, 0.35)
    ).astype(jnp.float32)
    diffusion_advance = diffusion_advance * (1.0 + 0.5 * jnp.tanh(archived_nominal_heat_levels))
    first_u = TIME_STEP * flux_perturbation / capacity[0, 0]
    second_top = TIME_STEP * flux_perturbation + TIME_STEP * (
        diffusion_advance[0, 0] * (surface_rim(first_u) - 6.0 * first_u) + flux_perturbation
    )
    second_low = TIME_STEP * diffusion_advance[0, 1] * first_u
    top_u = second_top / capacity[1, 0]
    low_u = second_low / capacity[1, 1]
    third_top = second_top + TIME_STEP * (
        diffusion_advance[1, 0] * (surface_rim(top_u) - 6.0 * top_u + low_u) + flux_perturbation
    )
    misfit = OBS_WEIGHT * third_top / capacity[1, 0]
    adj_three = misfit / capacity[1, 0]
    push_top = TIME_STEP * diffusion_advance[1, 0] * adj_three
    adj_two_top = adj_three + (surface_rim(push_top) - 6.0 * push_top) / capacity[1, 0]
    adj_two_low = push_top / capacity[1, 1]
    pull_top = TIME_STEP * diffusion_advance[0, 0] * adj_two_top
    pull_low = TIME_STEP * diffusion_advance[0, 1] * adj_two_low
    adj_one_top = adj_two_top + (surface_rim(pull_top) - 6.0 * pull_top + pull_low) / capacity[0, 0]
    return TIME_STEP * (adj_three + adj_two_top + adj_one_top)


def shards(q, heat, labels):
    nvec, bx, by = q.shape
    along, across = lax.axis_size("gy"), lax.axis_size("gx")
    rows, width = bx // along, by // across
    square = bx * across == by * along
    if not square or rows % 16 or width % 128 or by % (by * along // OUTER):
        return shards_general(q, heat, labels)
    return data_term(q, heat, labels) + prior(q)


def solution(mesh):
    in_specs = (P(None, "gx", "gy"), P(None, None, "gx", "gy"), P(None, None, "gx", "gy"))
    out_specs = P(None, "gx", "gy")
    return jax.shard_map(shards, mesh=mesh, in_specs=in_specs, out_specs=out_specs, check_vma=False)
```

```python
import math

import jax
import jax.numpy as jnp
import numpy as np
from jax import lax
from jax.experimental import pallas as pl
from jax.experimental.pallas import tpu as pltpu
from jax.sharding import PartitionSpec as P

TIME_STEP = 0.1
OBS_WEIGHT = 10.0
PRIOR_GAIN = 0.005
HIGHEST = lax.Precision.HIGHEST


def with_halo(cells, sides, width):
    for axis, dim in sides:
        count = lax.axis_size(axis)
        ends = count - 1
        head = lax.slice_in_dim(cells, 0, width, axis=dim)
        tail = lax.slice_in_dim(cells, cells.shape[dim] - width, cells.shape[dim], axis=dim)
        cells = jnp.concatenate(
            [
                lax.ppermute(tail, axis, [(i, (i + 1) % count) for i in range(ends)]),
                cells,
                lax.ppermute(head, axis, [((i + 1) % count, i) for i in range(ends)]),
            ],
            axis=dim,
        )
    return cells


def surface_rim(field):
    padded = with_halo(field, (("gx", 1), ("gy", 2)), 1)
    return padded[:, 2:, 1:-1] + padded[:, :-2, 1:-1] + padded[:, 1:-1, 2:] + padded[:, 1:-1, :-2]


def cos_sin(horizontal_line_total, col_count, modulus):
    row_ids = jnp.arange(horizontal_line_total, dtype=jnp.int32)[:, None]
    col_ids = jnp.arange(col_count, dtype=jnp.int32)[None, :]
    angles = (row_ids * col_ids % modulus).astype(jnp.float32) * (2.0 * math.pi / modulus)
    return (jnp.cos(angles), jnp.sin(angles))


def tables(length):
    bit_count = length.bit_length() - 1
    outer_len = 2 ** (bit_count // 2)
    inner_len = length // outer_len
    cos_outer, sin_outer = cos_sin(outer_len, outer_len, outer_len)
    cos_inner, sin_inner = cos_sin(inner_len, inner_len, inner_len)
    twist_cos, twist_sin = cos_sin(outer_len, inner_len, length)
    outer_fwd = jnp.stack([cos_outer, -sin_outer])
    inner_fwd = jnp.stack([jnp.stack([cos_inner, -sin_inner]), jnp.stack([sin_inner, cos_inner])])
    inner_inv = jnp.stack([jnp.stack([cos_inner, sin_inner]), jnp.stack([-sin_inner, cos_inner])])
    outer_inv = jnp.stack([cos_outer, -sin_outer])
    freq_index = (
        jnp.arange(outer_len, dtype=jnp.int32)[:, None]
        + outer_len * jnp.arange(inner_len, dtype=jnp.int32)[None, :]
    )
    signed = jnp.where(freq_index < length // 2, freq_index, freq_index - length).astype(
        jnp.float32
    )
    wave_sq = (signed * (2.0 * math.pi / length)) ** 2
    return (
        length,
        outer_len,
        inner_len,
        outer_fwd,
        inner_fwd,
        inner_inv,
        outer_inv,
        twist_cos,
        twist_sin,
        wave_sq,
    )


def forward(field, table):
    (
        length,
        outer_len,
        inner_len,
        outer_fwd,
        inner_fwd,
        inner_inv,
        outer_inv,
        twist_cos,
        twist_sin,
        wave_sq,
    ) = table
    grid = field.reshape(field.shape[:-1] + (outer_len, inner_len))
    stepped = jnp.einsum("...ab,rak->...rkb", grid, outer_fwd, precision=HIGHEST)
    step_re = stepped[..., 0, :, :]
    step_im = stepped[..., 1, :, :]
    twisted = jnp.stack(
        [step_re * twist_cos + step_im * twist_sin, step_im * twist_cos - step_re * twist_sin],
        axis=-3,
    )
    spec = jnp.einsum("...rkb,rsbm->...skm", twisted, inner_fwd, precision=HIGHEST)
    return (spec[..., 0, :, :], spec[..., 1, :, :])


def inverse(spec_re, spec_im, table):
    (
        length,
        outer_len,
        inner_len,
        outer_fwd,
        inner_fwd,
        inner_inv,
        outer_inv,
        twist_cos,
        twist_sin,
        wave_sq,
    ) = table
    stacked = jnp.stack([spec_re, spec_im], axis=-3)
    halved = jnp.einsum("...skm,srbm->...rkb", stacked, inner_inv, precision=HIGHEST)
    half_re = halved[..., 0, :, :]
    half_im = halved[..., 1, :, :]
    turned = jnp.stack(
        [half_re * twist_cos - half_im * twist_sin, half_im * twist_cos + half_re * twist_sin],
        axis=-3,
    )
    grid = jnp.einsum("...rkb,rka->...ab", turned, outer_inv, precision=HIGHEST)
    return grid.reshape(grid.shape[:-2] + (length,)) / length


def shards_general(flux_perturbation, archived_nominal_heat_levels, archived_solidity_labels):
    capacity = jnp.where(
        archived_solidity_labels == 0, 1.0, jnp.where(archived_solidity_labels == 1, 4.0, 1.25)
    ).astype(jnp.float32)
    diffusion_advance = jnp.where(
        archived_solidity_labels == 0, 1.0, jnp.where(archived_solidity_labels == 1, 0.6, 0.35)
    ).astype(jnp.float32)
    diffusion_advance = diffusion_advance * (1.0 + 0.5 * jnp.tanh(archived_nominal_heat_levels))
    rows = lax.all_to_all(flux_perturbation, "gx", split_axis=2, concat_axis=1, tiled=True)
    row_table = tables(rows.shape[1])
    first_u = TIME_STEP * flux_perturbation / capacity[0, 0]
    second_top = TIME_STEP * flux_perturbation + TIME_STEP * (
        diffusion_advance[0, 0] * (surface_rim(first_u) - 6.0 * first_u) + flux_perturbation
    )
    second_low = TIME_STEP * diffusion_advance[0, 1] * first_u
    top_u = second_top / capacity[1, 0]
    low_u = second_low / capacity[1, 1]
    third_top = second_top + TIME_STEP * (
        diffusion_advance[1, 0] * (surface_rim(top_u) - 6.0 * top_u + low_u) + flux_perturbation
    )
    misfit = OBS_WEIGHT * third_top / capacity[1, 0]
    adj_three = misfit / capacity[1, 0]
    push_top = TIME_STEP * diffusion_advance[1, 0] * adj_three
    adj_two_top = adj_three + (surface_rim(push_top) - 6.0 * push_top) / capacity[1, 0]
    adj_two_low = push_top / capacity[1, 1]
    pull_top = TIME_STEP * diffusion_advance[0, 0] * adj_two_top
    pull_low = TIME_STEP * diffusion_advance[0, 1] * adj_two_low
    adj_one_top = adj_two_top + (surface_rim(pull_top) - 6.0 * pull_top + pull_low) / capacity[0, 0]
    data_term = TIME_STEP * (adj_three + adj_two_top + adj_one_top)
    row_re, row_im = forward(jnp.swapaxes(rows, 1, 2), row_table)
    wave_x = row_table[-1]
    second_x = jnp.swapaxes(
        inverse(2.0 * PRIOR_GAIN * wave_x * row_re, 2.0 * PRIOR_GAIN * wave_x * row_im, row_table),
        1,
        2,
    )
    fourth_x = jnp.swapaxes(
        inverse(
            PRIOR_GAIN * wave_x * wave_x * row_re, PRIOR_GAIN * wave_x * wave_x * row_im, row_table
        ),
        1,
        2,
    )
    second_back, fourth_part = (
        lax.all_to_all(second_x, "gx", split_axis=1, concat_axis=2, tiled=True),
        lax.all_to_all(fourth_x, "gx", split_axis=1, concat_axis=2, tiled=True),
    )
    cols_dir, cols_second = (
        lax.all_to_all(flux_perturbation, "gy", split_axis=1, concat_axis=2, tiled=True),
        lax.all_to_all(second_back, "gy", split_axis=1, concat_axis=2, tiled=True),
    )
    col_table = tables(cols_dir.shape[2])
    dir_re, dir_im = forward(cols_dir, col_table)
    sec_re, sec_im = forward(cols_second, col_table)
    wave_y = col_table[-1]
    mixed = inverse(
        PRIOR_GAIN * wave_y * wave_y * dir_re + wave_y * sec_re,
        PRIOR_GAIN * wave_y * wave_y * dir_im + wave_y * sec_im,
        col_table,
    )
    mixed_back = lax.all_to_all(mixed, "gy", split_axis=2, concat_axis=1, tiled=True)
    return data_term + fourth_part + mixed_back


OUTER = 16


def half_spectrum(xs):
    n = len(xs)
    if n == 2:
        return [(xs[0] + xs[1], None), (xs[0] - xs[1], None)]
    even, odd = half_spectrum(xs[0::2]), half_spectrum(xs[1::2])
    out = [None] * (n // 2 + 1)
    for k in range(n // 4 + 1):
        er, ei = even[k]
        orr, oi = odd[k]
        if k == 0:
            out[0] = (er + orr, None)
            out[n // 2] = (er - orr, None)
        elif k == n // 4:
            out[k] = (er, -orr)
        else:
            c, s = math.cos(2 * math.pi * k / n), math.sin(2 * math.pi * k / n)
            if 8 * k == n:
                tr, ti = c * (orr + oi), c * (oi - orr)
            else:
                tr, ti = c * orr + s * oi, c * oi - s * orr
            out[k] = (er + tr, ei + ti)
            out[n // 2 - k] = (er - tr, ti - ei)
    return out


def half_spectrum_t(gs):
    half = len(gs) - 1
    n = 2 * half
    if n == 2:
        return [gs[0][0] + gs[1][0], gs[0][0] - gs[1][0]]
    even, odd = [], []
    for m in range(n // 4 + 1):
        gr, gi = gs[m]
        if m == 0:
            hr = gs[half][0]
            even.append((gr + hr, None))
            odd.append((gr - hr, None))
        elif m == n // 4:
            even.append((gr, None))
            odd.append((-gi, None))
        else:
            hr, hi = gs[half - m]
            even.append((gr + hr, gi - hi))
            dr, di = gr - hr, gi + hi
            c, s = math.cos(2 * math.pi * m / n), math.sin(2 * math.pi * m / n)
            if 8 * m == n:
                odd.append((c * (dr - di), c * (dr + di)))
            else:
                odd.append((c * dr - s * di, c * di + s * dr))
    out = [None] * n
    out[0::2] = half_spectrum_t(even)
    out[1::2] = half_spectrum_t(odd)
    return out


def line_tables(length):
    inner = length // OUTER
    groups = OUTER // 2
    b = np.arange(inner)[:, None]
    mats = np.zeros((groups, 2 * inner, 2 * inner))
    freq = np.zeros((groups, 2 * inner), np.int64)
    scale = math.sqrt(2.0 / length)
    for k1 in range(1, groups):
        k = k1 + OUTER * np.arange(inner)
        angle = 2.0 * math.pi * ((b * k[None, :]) % length) / length
        c, s = np.cos(angle) * scale, np.sin(angle) * scale
        mats[k1 - 1] = np.block([[c, -s], [s, c]])
        freq[k1 - 1] = np.concatenate([k, k])
    last = groups - 1
    for part, first in ((0, 0), (1, groups)):
        k = first + OUTER * np.arange(inner // 2)
        angle = 2.0 * math.pi * ((b * k[None, :]) % length) / length
        c, s = np.cos(angle) * scale, np.sin(angle) * scale
        k_sin = k.copy()
        if first == 0:
            c[:, 0] = math.sqrt(1.0 / length)
            k_sin[0] = length // 2
            s[:, 0] = -math.sqrt(1.0 / length) * (1 - 2 * (np.arange(inner) % 2))
        span = slice(part * inner, (part + 1) * inner)
        mats[last][span, span] = np.concatenate([c, -s], axis=1)
        freq[last][span] = np.concatenate([k, k_sin])
    signed = np.where(freq < length // 2, freq, freq - length)
    wave = (signed * (2.0 * math.pi / length)) ** 2
    return mats, wave


def two_parts(mats):
    top = np.asarray(mats, np.float32).astype(jnp.bfloat16)
    rest = (np.asarray(mats, np.float64) - top.astype(np.float64)).astype(jnp.bfloat16)
    return top, rest


def split(x):
    top = x.astype(jnp.bfloat16)
    return top, (x - top.astype(jnp.float32)).astype(jnp.bfloat16)


def dot32(a, b):
    return jnp.dot(a, b, preferred_element_type=jnp.float32)


def right(x, hi, lo):
    top, rest = split(x)
    return dot32(top, hi) + (dot32(rest, hi) + dot32(top, lo))


def left(hi, lo, x):
    top, rest = split(x)
    return dot32(hi, top) + (dot32(lo, top) + dot32(hi, rest))


def pairs(spec):
    ends = len(spec) - 1
    return [spec[k] for k in range(1, ends)] + [(spec[0][0], spec[ends][0])]


def unpairs(groups):
    return [(groups[-1][0], None)] + groups[:-1] + [(groups[-1][1], None)]


def y_forward(x_ref, hi_ref, lo_ref, out_ref):
    parts, wide = x_ref.shape[0], x_ref.shape[-1]
    inner = parts * wide // OUTER
    per = wide // inner
    xs = [x_ref[a // per, 0, :, (a % per) * inner : (a % per + 1) * inner] for a in range(OUTER)]
    width = out_ref.shape[-1]
    each = 2 * inner // width
    for g, (re, im) in enumerate(pairs(half_spectrum(xs))):
        res = right(jnp.concatenate([re, im], axis=1), hi_ref[g], lo_ref[g])
        for c in range(each):
            out_ref[g * each + c, 0] = res[:, c * width : (c + 1) * width]


def y_inverse(x_ref, hi_ref, lo_ref, out_ref):
    parts, wide = out_ref.shape[0], out_ref.shape[-1]
    inner = parts * wide // OUTER
    per = wide // inner
    width = x_ref.shape[-1]
    each = 2 * inner // width
    groups = []
    for g in range(OUTER // 2):
        spec = jnp.concatenate([x_ref[g * each + c, 0] for c in range(each)], axis=1)
        res = right(spec, hi_ref[g], lo_ref[g])
        groups.append((res[:, :inner], res[:, inner:]))
    for a, slab in enumerate(half_spectrum_t(unpairs(groups))):
        out_ref[a // per, 0, :, (a % per) * inner : (a % per + 1) * inner] = slab


def x_apply(x_ref, ky_ref, kx_ref, fhi_ref, flo_ref, ihi_ref, ilo_ref, out_ref):
    count, nvec, rows, width = x_ref.shape
    inner = count * rows // OUTER
    per = inner // rows

    def slab(a):
        return jnp.concatenate(
            [x_ref[a * per : (a + 1) * per, v].reshape(inner, width) for v in range(nvec)], axis=1
        )

    ky = jnp.concatenate([ky_ref[...]] * nvec, axis=1)
    groups = []
    for g, (re, im) in enumerate(pairs(half_spectrum([slab(a) for a in range(OUTER)]))):
        spec = left(fhi_ref[g], flo_ref[g], jnp.concatenate([re, im], axis=0))
        wave = kx_ref[g] + ky
        res = left(ihi_ref[g], ilo_ref[g], PRIOR_GAIN * wave * wave * spec)
        groups.append((res[:inner], res[inner:]))
    for a, res in enumerate(half_spectrum_t(unpairs(groups))):
        for v in range(nvec):
            out_ref[a * per : (a + 1) * per, v] = res[:, v * width : (v + 1) * width].reshape(
                per, rows, width
            )


def cost(flops, moved):
    return pl.CostEstimate(flops=int(flops), bytes_accessed=int(moved), transcendentals=0)


def prior(q, make_fields):
    across, along = lax.axis_size("gx"), lax.axis_size("gy")
    nvec, bx, by = q.shape
    length = by * along
    count = across * along
    rows = bx // along
    width = length // count
    mats, wave = line_tables(length)
    fhi, flo = two_parts(mats)
    thi, tlo = two_parts(np.swapaxes(mats, 1, 2))
    params = pltpu.CompilerParams(vmem_limit_bytes=VMEM_BYTES)
    lines_shape = jax.ShapeDtypeStruct((along, 1, rows, by), jnp.float32)
    packed_shape = jax.ShapeDtypeStruct((count, 1, rows, width), jnp.float32)
    work = 6 * mats.size * bx * by // length
    moved = 8 * bx * by + 4 * mats.size

    me = lax.axis_index("gx") * along + lax.axis_index("gy")
    ky = lax.dynamic_slice_in_dim(
        jnp.asarray(wave.reshape(1, length), jnp.float32), me * width, width, axis=1
    )
    kx = jnp.asarray(wave[:, :, None], jnp.float32)
    turns = range(nvec)
    whole_y = [
        lax.all_to_all(q[v].reshape(along, 1, rows, by), "gy", 0, 0, tiled=True) for v in turns
    ]
    spec_y = [
        pl.pallas_call(
            y_forward, out_shape=packed_shape, compiler_params=params, name="y_forward",
            cost_estimate=cost(work, moved),
        )(whole_y[v], fhi, flo)
        for v in turns
    ]
    spec_y[-1], fields = lax.optimization_barrier((spec_y[-1], make_fields()))
    whole_x = [lax.all_to_all(spec_y[v], ("gx", "gy"), 0, 0, tiled=True) for v in turns]
    done_x = [
        pl.pallas_call(
            x_apply, out_shape=packed_shape, compiler_params=params, name="x_apply",
            cost_estimate=cost(4 * work, 2 * moved),
        )(whole_x[v], ky, kx, thi, tlo, fhi, flo)
        for v in turns
    ]
    done_x[-1], fields = lax.optimization_barrier((done_x[-1], fields))
    data = data_part(fields, q)
    back_y = [lax.all_to_all(done_x[v], ("gx", "gy"), 0, 0, tiled=True) for v in turns]
    back_y[-1], data = lax.optimization_barrier((back_y[-1], data))
    done_y = [
        pl.pallas_call(
            y_inverse, out_shape=lines_shape, compiler_params=params, name="y_inverse",
            cost_estimate=cost(work, moved),
        )(back_y[v], thi, tlo)
        for v in turns
    ]
    back = [lax.all_to_all(done_y[v], "gy", 0, 0, tiled=True) for v in turns]
    return [back[v].reshape(bx, by) for v in turns], data


RIM = 8
VMEM_BYTES = 58 * 2**20


def shift(axis, step):
    count = lax.axis_size(axis)
    return [(i, i + step) for i in range(count) if 0 <= i + step < count]


def rims(q, heat, labels):
    bx, by = q.shape[1:]
    near = lambda cut: jnp.concatenate(
        [
            cut(q),
            (cut(labels) + 1).astype(jnp.float32).reshape((-1,) + cut(q).shape[1:]),
            cut(heat).reshape((-1,) + cut(q).shape[1:])[:-1],
        ]
    )
    above = lax.ppermute(near(lambda f: f[..., bx - RIM :, :]), "gx", shift("gx", 1))
    below = lax.ppermute(near(lambda f: f[..., :RIM, :]), "gx", shift("gx", -1))
    ends = []
    for cols, step in ((slice(0, RIM), -1), (slice(by - RIM, by), 1)):
        line = jnp.concatenate(
            [above[..., cols], near(lambda f: f[..., cols]), below[..., cols]], axis=1
        )
        line = lax.ppermute(jnp.swapaxes(line, 1, 2), "gy", shift("gy", step))
        ends.append(jnp.swapaxes(line, 1, 2))
    return above, below, ends[0], ends[1]


def widened(q, heat, labels, above, below, after, before):
    main = jnp.concatenate(
        [
            q,
            (labels + 1).astype(jnp.float32).reshape((-1,) + q.shape[1:]),
            heat.reshape((-1,) + q.shape[1:])[:-1],
        ]
    )
    tall = jnp.concatenate([above, main, below], axis=1)
    gap = jnp.zeros(tall.shape[:2] + (128 - 2 * RIM,), jnp.float32)
    return jnp.concatenate([tall, after, gap, before], axis=2)


def data_strips(f_ref, out_ref):
    nvec, bx, by = out_ref.shape
    strip = 32
    tall, wide = strip + 2 * RIM, f_ref.shape[2]

    def rim(f):
        return (pltpu.roll(f, 1, 0) + pltpu.roll(f, tall - 1, 0)) + (
            pltpu.roll(f, 1, 1) + pltpu.roll(f, wide - 1, 1)
        )

    def one(s, carry):
        first = pl.multiple_of(s * strip, strip)
        field = lambda i: f_ref[i, pl.ds(first, tall), :]

        def inverse_capacity(label):
            return jnp.where(label == 2.0, 0.25, jnp.where(label == 3.0, 0.8, 1.0))

        def conduct(label, level):
            base = jnp.where(
                label == 1.0, 1.0, jnp.where(label == 2.0, 0.6, jnp.where(label == 3.0, 0.35, 0.0))
            )
            return TIME_STEP * base * (1.0 + 0.5 * jnp.tanh(level))

        label = [field(nvec + i) for i in range(4)]
        ic_top0, ic_top1 = inverse_capacity(label[0]), inverse_capacity(label[2])
        ic_low1 = inverse_capacity(label[3])
        c_top0 = conduct(label[0], field(nvec + 4))
        c_low0 = conduct(label[1], field(nvec + 5))
        c_top1 = conduct(label[2], field(nvec + 6))
        for v in range(nvec):
            q = field(v)
            first_u = TIME_STEP * q * ic_top0
            second_top = (2.0 * TIME_STEP) * q + c_top0 * (rim(first_u) - 6.0 * first_u)
            top_u = second_top * ic_top1
            low_u = c_low0 * first_u * ic_low1
            third_top = (
                second_top + c_top1 * (rim(top_u) - 6.0 * top_u + low_u) + TIME_STEP * q
            )
            adj_three = OBS_WEIGHT * third_top * ic_top1 * ic_top1
            push_top = c_top1 * adj_three
            adj_two = adj_three + (rim(push_top) - 6.0 * push_top) * ic_top1
            pull_top = c_top0 * adj_two
            pull_low = c_low0 * (push_top * ic_low1)
            adj_one = adj_two + (rim(pull_top) - 6.0 * pull_top + pull_low) * ic_top0
            total = TIME_STEP * (adj_three + adj_two + adj_one)
            out_ref[v, pl.ds(first, strip), :] = total[RIM : RIM + strip, :by]
        return carry

    lax.fori_loop(0, bx // strip, one, 0)


def data_part(fields, like):
    return pl.pallas_call(
        data_strips,
        out_shape=jax.ShapeDtypeStruct(like.shape, jnp.float32),
        compiler_params=pltpu.CompilerParams(vmem_limit_bytes=VMEM_BYTES),
        cost_estimate=cost(400 * like.size, 4 * fields.size + 4 * like.size),
        name="data_strips",
    )(fields)


def shards(q, heat, labels):
    nvec, bx, by = q.shape
    along, across = lax.axis_size("gy"), lax.axis_size("gx")
    rows, width = bx // along, by // across
    square = bx * across == by * along
    if not square or rows % 16 or width % 128 or by % (by * along // OUTER) or bx % 32:
        return shards_general(q, heat, labels)
    q, *beyond = lax.optimization_barrier((q, *rims(q, heat, labels)))
    parts, data = prior(q, lambda: widened(q, heat, labels, *beyond))
    return jnp.stack([data[v] + part for v, part in enumerate(parts)])


def solution(mesh):
    in_specs = (P(None, "gx", "gy"), P(None, None, "gx", "gy"), P(None, None, "gx", "gy"))
    out_specs = P(None, "gx", "gy")
    return jax.shard_map(shards, mesh=mesh, in_specs=in_specs, out_specs=out_specs, check_vma=False)
```
